32 devices in a mesh: grp: 2 (over y), doc: 4 (over z), qry: 2 (over x), dim: 2 (over core).
Axes of the slice: x: 2, y: 2, z: 4, core: 2. Of those that a mesh axis runs over, the one named last changes fastest.
Arguments:
- queries: bfloat16 [8, 64, 32, 128], P(('grp', 'doc'), ('qry', 'dim')), parts along dimension 0, may hold values from -0.59765625 to 0.59765625
- codebook: bfloat16 [16384, 128], P(('qry', 'dim')), may hold values from -0.5 to 0.5
- bucket_values: float32 [4], replicated, may hold values from -0.12 to 0.12
- token_centroids: int32 [32768], P(('grp', 'doc')), parts along dimension 0, may hold values from 0 to 16383, as said below
- residual_codes: int32 [32768, 128], P(('grp', 'doc')), parts along dimension 0, may hold values from 0 to 3
- doc_blocks: int32 [8, 16], P(('grp', 'doc')), parts along dimension 0, may hold values from 1 to 20, 64 in all within a row
- cand_blocks: int32 [8, 4, 4, 32], P('grp', ('qry', 'dim'), 'doc'), parts along dimension 0, may hold values from 0 to 63
- cand_counts: int32 [8, 4, 4], P('grp', ('qry', 'dim'), 'doc'), parts along dimension 0, may hold values from 1 to 32, as said below
Outputs:
- scores: float32 [8, 64, 64], P('grp', ('qry', 'dim'), 'doc'), parts along dimension 0
The draws below stay inside these ranges and needn't reach their ends.
There are 2 independent parts, one for each index of `grp`. The reference program is written for one: setup_inputs(seed, part) draws one part's arguments, and reference() takes and returns one part's arrays. A program takes and returns all parts, laid end to end along the dimension named above; an argument that names none is the same for every part. Nothing has to cross between parts.
Inputs may be any that keep to these rules, and one draw needn't show every extreme that they name: `doc_blocks`: each row sums to 64. Slots from cand_counts on are ignored; some entry equals 32 in every draw. `token_centroids`: in each aligned run of 1024 tokens, exactly 256 have their centroid in each aligned range of 4096 codebook rows.
All inputs are finite; a program needn't handle non-finite values.
Results may differ from the reference program's by a relative error of at most 0.0003.
Values may be sent and summed in bfloat16 or wider, within the bound.
A program may use at most 64 MiB of HBM per device.

```python
import math
import jax
import jax.numpy as jnp
import numpy as np
from jax import lax

D = 128
QTOK = 32
BLOCK = 64
BUCKETS = 4
CPD = 4096
QP = 16
CB = 32
NBLK = 64
CYCLE = 4
KP = 4
QROWS = 64
CENT = 16384
NDS = 16
DOCMOST = 20
DOCTOK = 16384
SHARE = 1024


def draw_cand_counts(key, part):
    key = jax.random.fold_in(key, 7)
    subkeys = jax.random.split(key, 4)
    heavy = jax.random.randint(subkeys[0], (1, 1, CYCLE), 0, 2)
    lower = jax.random.randint(subkeys[1], (CYCLE, KP, CYCLE), 1, CB // 2 + 1)
    upper = jax.random.randint(subkeys[2], (CYCLE, KP, CYCLE), CB // 2 + 1, CB + 1)
    picked = jnp.where(heavy == 1, upper, lower).reshape(-1)
    where_full = jax.random.randint(subkeys[3], (), 0, CYCLE * KP * CYCLE)
    picked = picked.at[where_full].set(CB)
    return picked.reshape(CYCLE, KP, CYCLE).astype(jnp.int32)


def draw_token_centroids(key, part):
    key = jax.random.fold_in(key, 11)
    subkeys = jax.random.split(key, 2)
    share_count = DOCTOK // SHARE
    share_keys = jax.random.split(subkeys[0], share_count)
    shuffled = jax.vmap(lambda k: jax.random.permutation(k, SHARE))(share_keys)
    owners = shuffled % KP
    within = jax.random.randint(subkeys[1], (share_count, SHARE), 0, CPD)
    return (owners * CPD + within).reshape(DOCTOK).astype(jnp.int32)


def place_ends(values, stream_key, least, top_value):
    longest = values.shape.index(max(values.shape))
    spots = []
    for shift in (0, 1):
        where = [jax.random.randint(jax.random.fold_in(stream_key, axis), (), 0, length) for axis, length in enumerate(values.shape)]
        where[longest] = (where[longest] + shift) % values.shape[longest]
        spots.append(tuple(where))
    return values.at[spots[0]].set(least).at[spots[1]].set(top_value)


def shard_levels(stream_key, dims, cuts, low, top_value):
    level = 1.0
    for position, shards_of in cuts:
        heights = jax.random.uniform(jax.random.fold_in(jax.random.fold_in(stream_key, 6), position), (shards_of,), jnp.float32, low / len(cuts), top_value / len(cuts))
        level = level * jnp.repeat(jnp.exp(heights), dims[position] // shards_of).reshape((-1,) + (1,) * (len(dims) - 1 - position))
    return level


def length_profile(count, total, limit, skew):
    loads = [(1 << 20) // math.isqrt(rank ** skew) + 1 for rank in range(2, count + 1)]
    spare, counts = total - limit - (count - 1), [1] * (count - 1)
    while spare > 0:
        candidates = [i for i in range(count - 1) if counts[i] < limit]
        mass, left = sum([loads[i] for i in candidates]), spare
        for i in candidates:
            extra = min(limit - counts[i], max(1, left * loads[i] // mass), spare)
            counts[i] = counts[i] + extra
            spare = spare - extra
    return np.array([limit] + counts)


def ragged(own_key, amount, total, limit, skew):
    if amount == 2:
        one = jax.random.randint(own_key, (), max(1, total - limit), min(limit, total - 1) + 1)
        return jnp.stack([one, total - one])
    sizes = jnp.asarray(length_profile(amount, total, limit, skew), jnp.int32)
    couples = (amount - 1) // 2
    source_of, receiver = sizes[1:1 + 2 * couples:2], sizes[2:2 + 2 * couples:2]
    margin = jnp.minimum(source_of - 1, limit - receiver)
    passed = jax.random.randint(jax.random.fold_in(own_key, 1), (couples,), 0, 1 << 20) % (margin + 1)
    sizes = sizes.at[1:1 + 2 * couples:2].set(source_of - passed).at[2:2 + 2 * couples:2].set(receiver + passed)
    return sizes[jax.random.permutation(jax.random.fold_in(own_key, 2), amount)]


def scatter_about(own_key, extent, width, limit, shards=(), kind=jnp.bfloat16):
    level = shard_levels(own_key, extent, shards, -0.22, 0.18) if shards else 1.0
    entries = jax.random.normal(own_key, extent, jnp.float32) * width * level
    return jnp.minimum(jnp.maximum(entries, -limit), limit).astype(kind)


def setup_inputs(seed: int = 0, part: int = 0) -> dict:
    keys = jax.random.split(jax.random.key(seed), 9)
    own_keys = jax.random.split(jax.random.fold_in(keys[8], part), 9)
    queries = scatter_about(own_keys[0], (CYCLE, QROWS, QTOK, D), 0.088, 0.59765625, ((0, 4), (1, 4)))
    codebook = scatter_about(keys[1], (CENT, D), D ** -0.5, 0.5, ((0, 4),))
    bucket_values = jnp.clip(jax.random.uniform(keys[2], (BUCKETS,), jnp.float32, -0.12, 0.12), -0.12, 0.12)
    token_centroids = draw_token_centroids(jax.random.fold_in(jax.random.fold_in(keys[8], part), 71), part)
    residual_codes = place_ends(jax.random.randint(own_keys[4], (DOCTOK, D), 0, BUCKETS), jax.random.fold_in(own_keys[4], 1), 0, BUCKETS - 1).astype(jnp.int32)
    doc_blocks = jax.vmap(lambda own: ragged(own, NDS, NBLK, DOCMOST, 1))(jax.random.split(own_keys[5], CYCLE)).reshape((CYCLE, NDS)).astype(jnp.int32)
    cand_blocks = place_ends(jax.random.randint(own_keys[6], (CYCLE, KP, CYCLE, CB), 0, NBLK), jax.random.fold_in(own_keys[6], 1), 0, NBLK - 1).astype(jnp.int32)
    cand_counts = draw_cand_counts(jax.random.fold_in(jax.random.fold_in(keys[8], part), 71), part)
    return dict(queries=queries, codebook=codebook, bucket_values=bucket_values, token_centroids=token_centroids, residual_codes=residual_codes, doc_blocks=doc_blocks, cand_blocks=cand_blocks, cand_counts=cand_counts)


norm_eps = 1e-06
floor_value = -10000.0

def decode_tokens(codebook, bucket_values, token_centroids, residual_codes):
    centroid = jnp.take(codebook, token_centroids, axis=0).astype(jnp.float32)
    vectors = centroid + jnp.take(bucket_values, residual_codes)
    scaled = vectors / jnp.sqrt(lax.optimization_barrier(jnp.sum(vectors * vectors, axis=-1, keepdims=True)) + norm_eps)
    return scaled.astype(jnp.bfloat16)

def score_panel(panel_now, decoded_blocks, slot_ids, live_count, block_doc):
    flat_q = panel_now.reshape(-1, panel_now.shape[-1])
    chosen = jnp.take(decoded_blocks, slot_ids, axis=0).reshape(-1, panel_now.shape[-1])
    similar = jnp.dot(flat_q, chosen.T, preferred_element_type=jnp.float32)
    tokens_max = similar.reshape(flat_q.shape[0], slot_ids.shape[0], -1).max(axis=2)
    alive_slots = jnp.arange(slot_ids.shape[0], dtype=jnp.int32) < live_count
    slot_doc = jnp.take(block_doc, slot_ids)
    member = (slot_doc[:, None] == jnp.arange(NDS, dtype=jnp.int32)[None, :]) & alive_slots[:, None]
    best_max = lax.optimization_barrier(jnp.max(jnp.where(member[None], tokens_max[:, :, None], floor_value), axis=1))
    present = jnp.any(member, axis=0)
    masked = jnp.where(present[None], best_max, 0.0)
    return masked.reshape(panel_now.shape[0], panel_now.shape[1], NDS).sum(axis=1) / QTOK

def reference(queries, codebook, bucket_values, token_centroids, residual_codes, doc_blocks, cand_blocks, cand_counts):
    decoded = decode_tokens(codebook, bucket_values, token_centroids, residual_codes)
    decoded = decoded.reshape(CYCLE, NBLK, BLOCK * D)
    doc_ends = jnp.cumsum(doc_blocks, axis=1)
    block_doc = lax.optimization_barrier(jnp.sum(doc_ends[:, None, :] <= jnp.arange(NBLK, dtype=jnp.int32)[None, :, None], axis=2)).astype(jnp.int32)
    panels = queries.reshape(CYCLE, KP, QP, QTOK, D)

    def per_shard(shard):

        def per_panel(index):
            row = index // KP
            col = index % KP
            return score_panel(panels[row, col], decoded[shard], cand_blocks[row, col, shard], cand_counts[row, col, shard], block_doc[shard])
        return lax.map(per_panel, jnp.arange(CYCLE * KP, dtype=jnp.int32))
    result = lax.map(per_shard, jnp.arange(CYCLE, dtype=jnp.int32))
    result = result.reshape(CYCLE, CYCLE, KP, QP, NDS).transpose(1, 2, 3, 0, 4)
    return result.reshape(CYCLE, KP * QP, CYCLE * NDS)
```

```python
import functools

import jax
import jax.numpy as jnp
from jax import lax
from jax.experimental import pallas as pl
from jax.experimental.pallas import tpu as pltpu
from jax.sharding import PartitionSpec as P

BLOCK = 64
LANES = 128
ROWS = 8
SUPER = ROWS * LANES

norm_eps = 1e-06
floor_value = -10000.0
bf16, f32, i32 = jnp.bfloat16, jnp.float32, jnp.int32


def kernel(
    shards, owners_x, cores,
    ids_ref, cand_ref, counts_ref, docs_ref, bucket_ref, q_ref, book_hbm, codes_hbm,
    out_ref,
    book, codes, ranks, place, slots, rows, perm, resid, dec, panels, best,
    load_sem, q_send, q_recv, x_send, c_send, r_send, row_recv,
):
    y, z = lax.axis_index("grp"), lax.axis_index("doc")
    x, c = lax.axis_index("qry"), lax.axis_index("dim")
    owners = owners_x * cores
    me = x * cores + c
    held = book.shape[0]
    supers = codes.shape[0] // SUPER
    width = SUPER // owners
    run_rows = codes.shape[0] // owners // LANES
    part = SUPER // (run_rows * LANES)
    share = width // part
    token_rows = ids_ref.shape[0]

    load_book = pltpu.make_async_copy(book_hbm, book, load_sem.at[0])
    load_codes = pltpu.make_async_copy(codes_hbm, codes, load_sem.at[1])
    load_book.start()
    load_codes.start()

    barrier = pltpu.get_barrier_semaphore()
    peers = [(y, lax.rem(z + s, shards), x, c) for s in range(1, shards)]
    peers += [(y, z, lax.rem(x + s, owners_x), c) for s in range(1, owners_x)]
    peers += [(y, z, x, lax.rem(c + s, cores)) for s in range(1, cores)]
    for peer in peers:
        pl.semaphore_signal(barrier, inc=1, device_id=peer, device_id_type=pl.DeviceIdType.MESH)

    ids = ids_ref[...]
    owner = ids // held
    lane_r = lax.broadcasted_iota(i32, (LANES, LANES), 0)
    lane_c = lax.broadcasted_iota(i32, (LANES, LANES), 1)
    before = (lane_r < lane_c).astype(bf16)
    ones = jnp.ones((LANES, LANES), bf16)
    row_r = lax.broadcasted_iota(i32, (token_rows, token_rows), 0)
    row_c = lax.broadcasted_iota(i32, (token_rows, token_rows), 1)
    above = ((row_c < row_r) & (row_c // run_rows == row_r // run_rows)).astype(bf16)
    rank = jnp.zeros(ids.shape, f32)
    for o in range(owners):
        mask = (owner == o).astype(f32)
        inside = jnp.dot(mask.astype(bf16), before, preferred_element_type=f32)
        totals = jnp.dot(mask.astype(bf16), ones, preferred_element_type=f32)
        carried = jnp.dot(above, totals.astype(bf16), preferred_element_type=f32)
        rank = rank + mask * (inside + carried)
    run_of = (lax.broadcasted_iota(i32, ids.shape, 0) // run_rows) % part
    slot = run_of * share + rank.astype(i32)
    place[...] = owner * width + slot
    slots[...] = jnp.where(owner == me, slot, -1)
    ranks[...] = ids - me * held

    pl.semaphore_wait(barrier, len(peers))

    def q_copy(s):
        return pltpu.make_async_remote_copy(
            src_ref=q_ref, dst_ref=panels.at[z],
            send_sem=q_send.at[s], recv_sem=q_recv.at[z],
            device_id=(y, lax.rem(z + s, shards), x, c), device_id_type=pl.DeviceIdType.MESH,
        )

    for s in range(1, shards):
        q_copy(s).start()

    def chunk(q, o):
        return rows.at[q, pl.ds(pl.multiple_of(o * width, width), width), :]

    def send(q, o, sem, device):
        return pltpu.make_async_remote_copy(
            src_ref=chunk(q, o), dst_ref=chunk(q, o), send_sem=sem, recv_sem=row_recv.at[q, o],
            device_id=device, device_id_type=pl.DeviceIdType.MESH,
        )

    def x_copy(q, s):
        return send(q, me, x_send.at[q, s], (y, z, lax.rem(x + s, owners_x), c))

    def c_copy(q, s):
        return send(q, me, c_send.at[q, s], (y, z, x, lax.rem(c + s, cores)))

    def relay(q, s, t):
        source = lax.rem(x + s, owners_x) * cores + c
        return send(q, source, r_send.at[q, s, t], (y, z, x, lax.rem(c + t, cores)))

    load_book.wait()
    spot = lax.broadcasted_iota(i32, (width, LANES), 0)
    held_iota = lax.broadcasted_iota(i32, (width, held), 1)

    def pick(q, _):
        slot_q = slots[pl.ds(pl.multiple_of(q * ROWS, ROWS), ROWS), :]
        id_q = ranks[pl.ds(pl.multiple_of(q * ROWS, ROWS), ROWS), :]
        total = jnp.zeros((width, LANES), i32)
        for s in range(ROWS):
            total = total + jnp.where(slot_q[s:s + 1, :] == spot, id_q[s:s + 1, :], 0)
        chosen = jnp.sum(total.astype(f32), axis=1, keepdims=True).astype(i32)
        hot = jnp.where(held_iota == chosen, 1.0, 0.0).astype(bf16)
        picked = jnp.dot(hot, book[...], preferred_element_type=f32).astype(bf16)
        rows[q, pl.ds(pl.multiple_of(me * width, width), width), :] = picked
        for s in range(1, owners_x):
            x_copy(q, s).start()
        for s in range(1, cores):
            c_copy(q, s).start()
        return 0

    lax.fori_loop(0, supers, pick, 0)

    load_codes.wait()
    levels = [bucket_ref[v] for v in range(bucket_ref.shape[0])]
    place_iota = lax.broadcasted_iota(i32, (2 * ROWS, SUPER), 1)

    def prepare(q, _):
        place_q = place[pl.ds(pl.multiple_of(q * ROWS, ROWS), ROWS), :]
        for l in range(0, LANES, 2):
            pair = jnp.concatenate([place_q[:, l:l + 1], place_q[:, l + 1:l + 2]], axis=0)
            perm[q, l * ROWS:(l + 2) * ROWS, :] = jnp.where(place_iota == pair, 1.0, 0.0).astype(bf16)
        for l in range(LANES):
            code = codes[pl.ds(q * SUPER + l, ROWS, stride=LANES), :]
            value = jnp.full(code.shape, levels[0], f32)
            for v in range(1, len(levels)):
                value = jnp.where(code == v, levels[v], value)
            resid[q, l * ROWS:(l + 1) * ROWS, :] = value
        for s in range(1, owners_x):
            source = lax.rem(x + s, owners_x) * cores + c
            x_wait = send(q, source, x_send.at[q, s], (y, z, x, c))
            x_wait.wait_recv()
            for t in range(1, cores):
                relay(q, s, t).start()
        return 0

    lax.fori_loop(0, supers, prepare, 0)

    blocks = supers * 2 * ROWS
    line = lax.broadcasted_iota(i32, (blocks, 1), 0)
    block = 2 * ROWS * (line // (2 * ROWS)) + 2 * (line % ROWS) + (line // ROWS) % 2
    end = jnp.int32(0)
    doc = jnp.zeros((blocks, 1), i32)
    docs = docs_ref.shape[1]
    for d in range(docs):
        end = end + docs_ref[0, d]
        doc = doc + jnp.where(end <= block, 1, 0)

    def score(j, query, q):
        for h in range(2):
            top = None
            for p in range(0, BLOCK * ROWS, 128):
                piece = dec[q, h * BLOCK * ROWS + p:h * BLOCK * ROWS + p + 128, :]
                sim = lax.dot_general(piece, query, (((1,), (1,)), ((), ())), preferred_element_type=f32)
                sim = jnp.max(sim.reshape(-1, ROWS, sim.shape[1]), axis=0)
                top = sim if top is None else jnp.maximum(top, sim)
            best[j, pl.ds(pl.multiple_of(q * 2 * ROWS + h * ROWS, ROWS), ROWS), :] = top

    def decode(q, _):
        for s in range(owners_x):
            for t in range(cores):
                if t == 0:
                    continue
                source = lax.rem(x + s, owners_x) * cores + lax.rem(c + t, cores)
                send(q, source, c_send.at[q, t], (y, z, x, c)).wait_recv()
        vectors = jnp.dot(perm[q], rows[q], preferred_element_type=f32) + resid[q]
        squares = jnp.sum(vectors * vectors, axis=1, keepdims=True)
        dec[q] = (vectors * lax.rsqrt(squares + norm_eps)).astype(bf16)
        score(z, q_ref[...], q)
        return 0

    lax.fori_loop(0, supers, decode, 0)

    panel_rows = q_ref.shape[0]
    queries = out_ref.shape[1]
    tokens = panel_rows // queries
    gather = (
        lax.broadcasted_iota(i32, (queries, panel_rows), 1) // tokens
        == lax.broadcasted_iota(i32, (queries, panel_rows), 0)
    ).astype(f32)
    slot_count = cand_ref.shape[3]
    slot_iota = lax.broadcasted_iota(i32, (1, slot_count), 1)

    def finish(j):
        live = (cand_ref[j, 0] == block) & (slot_iota < counts_ref[j, 0, 0])
        alive = jnp.max(jnp.where(live, 1.0, 0.0), axis=1, keepdims=True) > 0.5
        which = jnp.where(alive, doc, -1)
        maxima = best[j]
        lines = []
        for d in range(docs):
            lines.append(jnp.max(jnp.where(which == d, maxima, floor_value), axis=0, keepdims=True))
        found = jnp.concatenate(lines, axis=0)
        found = jnp.where(found > 0.5 * floor_value, found, 0.0)
        total = lax.dot_general(
            gather, found, (((1,), (1,)), ((), ())),
            preferred_element_type=f32, precision=lax.Precision.HIGHEST,
        )
        out_ref[j] = total * (1.0 / tokens)

    finish(z)

    def panel(s, _):
        j = lax.rem(z + shards - s, shards)
        pltpu.make_async_remote_copy(
            src_ref=q_ref, dst_ref=panels.at[j], send_sem=q_send.at[s], recv_sem=q_recv.at[j],
            device_id=(y, z, x, c), device_id_type=pl.DeviceIdType.MESH,
        ).wait_recv()

        def each(q, _):
            score(j, panels[j], q)
            return 0

        lax.fori_loop(0, supers, each, 0)
        finish(j)
        return 0

    lax.fori_loop(1, shards, panel, 0)

    for s in range(1, shards):
        q_copy(s).wait_send()

    def drain(q, _):
        for s in range(1, owners_x):
            x_copy(q, s).wait_send()
            for t in range(1, cores):
                relay(q, s, t).wait_send()
        for s in range(1, cores):
            c_copy(q, s).wait_send()
        return 0

    lax.fori_loop(0, supers, drain, 0)


def local(shards, owners_x, cores, queries, codebook, bucket_values, token_centroids, residual_codes,
          doc_blocks, cand_blocks, cand_counts):
    count, panel, tokens, depth = queries.shape[0], queries.shape[1], queries.shape[2], queries.shape[3]
    flat_q = queries.reshape(panel * tokens, depth)
    total = token_centroids.shape[0]
    supers = total // SUPER
    held = codebook.shape[0]
    owners = owners_x * cores
    docs = doc_blocks.shape[1]
    vmem, smem = pl.BlockSpec(memory_space=pltpu.VMEM), pl.BlockSpec(memory_space=pltpu.SMEM)
    anywhere = pl.BlockSpec(memory_space=pl.ANY)
    dma = pltpu.SemaphoreType.DMA
    return pl.pallas_call(
        functools.partial(kernel, shards, owners_x, cores),
        out_shape=jax.ShapeDtypeStruct((shards, panel, docs), f32),
        in_specs=[vmem, vmem, smem, smem, smem, vmem, anywhere, anywhere],
        out_specs=vmem,
        scratch_shapes=[
            pltpu.VMEM((held, depth), bf16),
            pltpu.VMEM((total, depth), i32),
            pltpu.VMEM((total // LANES, LANES), i32),
            pltpu.VMEM((total // LANES, LANES), i32),
            pltpu.VMEM((total // LANES, LANES), i32),
            pltpu.VMEM((supers, SUPER, depth), bf16),
            pltpu.VMEM((supers, SUPER, SUPER), bf16),
            pltpu.VMEM((supers, SUPER, depth), f32),
            pltpu.VMEM((supers, SUPER, depth), bf16),
            pltpu.VMEM((shards, panel * tokens, depth), bf16),
            pltpu.VMEM((shards, total // BLOCK, panel * tokens), f32),
            dma((2,)),
            dma((shards,)),
            dma((shards,)),
            dma((supers, owners_x)),
            dma((supers, cores)),
            dma((supers, owners_x, cores)),
            dma((supers, owners)),
        ],
        compiler_params=pltpu.CompilerParams(
            collective_id=0, has_side_effects=True, vmem_limit_bytes=50 * 1024 * 1024
        ),
        name="rescore",
    )(
        token_centroids.reshape(total // LANES, LANES), cand_blocks, cand_counts, doc_blocks,
        bucket_values, flat_q, codebook, residual_codes,
    )


def solution(mesh):
    in_specs = (
        P(("grp", "doc"), ("qry", "dim"), None, None),
        P(("qry", "dim"), None),
        P(),
        P(("grp", "doc")),
        P(("grp", "doc"), None),
        P(("grp", "doc"), None),
        P("grp", ("qry", "dim"), "doc", None),
        P("grp", ("qry", "dim"), "doc"),
    )
    out_specs = P("grp", ("qry", "dim"), "doc")
    body = functools.partial(local, mesh.shape["doc"], mesh.shape["qry"], mesh.shape["dim"])
    return jax.shard_map(body, mesh=mesh, in_specs=in_specs, out_specs=out_specs, check_vma=False)
```

```python
import functools

import jax
import jax.numpy as jnp
from jax import lax
from jax.experimental import pallas as pl
from jax.experimental.pallas import tpu as pltpu
from jax.sharding import PartitionSpec as P

BLOCK = 64
LANES = 128
ROWS = 8
SUPER = ROWS * LANES

norm_eps = 1e-06
floor_value = -10000.0
bf16, f32, i32 = jnp.bfloat16, jnp.float32, jnp.int32


def kernel(
    shards, owners_x, cores,
    ids_hbm, cand_hbm, counts_hbm, docs_hbm, bucket_hbm, q_hbm, book_hbm, codes_hbm,
    out_ref,
    ids_ref, cand_ref, counts_ref, docs_ref, bucket_ref, q_ref, book, codes, ranks, place, slots, rows, perm, resid, dec, panels, best,
    load_sem, q_send, q_recv, x_send, c_send, r_send, row_recv,
):
    y, z = lax.axis_index("grp"), lax.axis_index("doc")
    x, c = lax.axis_index("qry"), lax.axis_index("dim")
    owners = owners_x * cores
    me = x * cores + c
    held = book.shape[0]
    supers = codes.shape[0] // SUPER
    width = SUPER // owners
    run_rows = codes.shape[0] // owners // LANES
    part = SUPER // (run_rows * LANES)
    share = width // part
    token_rows = ids_ref.shape[0]

    loads = [
        pltpu.make_async_copy(source, target, load_sem.at[n])
        for n, (source, target) in enumerate([
            (ids_hbm, ids_ref), (q_hbm, q_ref), (book_hbm, book), (codes_hbm, codes), (cand_hbm, cand_ref),
            (counts_hbm, counts_ref), (docs_hbm, docs_ref), (bucket_hbm, bucket_ref),
        ])
    ]
    load_ids, load_q, load_book, load_codes = loads[:4]
    for load in loads:
        load.start()

    barrier = pltpu.get_barrier_semaphore()
    peers = [(y, lax.rem(z + s, shards), x, c) for s in range(1, shards)]
    peers += [(y, z, lax.rem(x + s, owners_x), c) for s in range(1, owners_x)]
    peers += [(y, z, x, lax.rem(c + s, cores)) for s in range(1, cores)]
    for peer in peers:
        pl.semaphore_signal(barrier, inc=1, device_id=peer, device_id_type=pl.DeviceIdType.MESH)

    load_ids.wait()
    ids = ids_ref[...]
    owner = ids // held
    lane_r = lax.broadcasted_iota(i32, (LANES, LANES), 0)
    lane_c = lax.broadcasted_iota(i32, (LANES, LANES), 1)
    before = (lane_r < lane_c).astype(bf16)
    ones = jnp.ones((LANES, LANES), bf16)
    row_r = lax.broadcasted_iota(i32, (token_rows, token_rows), 0)
    row_c = lax.broadcasted_iota(i32, (token_rows, token_rows), 1)
    above = ((row_c < row_r) & (row_c // run_rows == row_r // run_rows)).astype(bf16)
    rank = jnp.zeros(ids.shape, f32)
    for o in range(owners):
        mask = (owner == o).astype(f32)
        inside = jnp.dot(mask.astype(bf16), before, preferred_element_type=f32)
        totals = jnp.dot(mask.astype(bf16), ones, preferred_element_type=f32)
        carried = jnp.dot(above, totals.astype(bf16), preferred_element_type=f32)
        rank = rank + mask * (inside + carried)
    run_of = (lax.broadcasted_iota(i32, ids.shape, 0) // run_rows) % part
    slot = run_of * share + rank.astype(i32)
    place[...] = owner * width + slot
    slots[...] = jnp.where(owner == me, slot, -1)
    ranks[...] = ids - me * held

    load_q.wait()
    pl.semaphore_wait(barrier, len(peers))

    def q_copy(s):
        return pltpu.make_async_remote_copy(
            src_ref=q_ref, dst_ref=panels.at[z],
            send_sem=q_send.at[s], recv_sem=q_recv.at[z],
            device_id=(y, lax.rem(z + s, shards), x, c), device_id_type=pl.DeviceIdType.MESH,
        )

    for s in range(1, shards):
        q_copy(s).start()

    def chunk(q, o):
        return rows.at[q, pl.ds(pl.multiple_of(o * width, width), width), :]

    def send(q, o, sem, device):
        return pltpu.make_async_remote_copy(
            src_ref=chunk(q, o), dst_ref=chunk(q, o), send_sem=sem, recv_sem=row_recv.at[q, o],
            device_id=device, device_id_type=pl.DeviceIdType.MESH,
        )

    def x_copy(q, s):
        return send(q, me, x_send.at[q, s], (y, z, lax.rem(x + s, owners_x), c))

    def c_copy(q, s):
        return send(q, me, c_send.at[q, s], (y, z, x, lax.rem(c + s, cores)))

    def relay(q, s, t):
        source = lax.rem(x + s, owners_x) * cores + c
        return send(q, source, r_send.at[q, s, t], (y, z, x, lax.rem(c + t, cores)))

    load_book.wait()
    spot = lax.broadcasted_iota(i32, (width, LANES), 0)
    held_iota = lax.broadcasted_iota(i32, (width, held), 1)

    def pick(q, _):
        slot_q = slots[pl.ds(pl.multiple_of(q * ROWS, ROWS), ROWS), :]
        id_q = ranks[pl.ds(pl.multiple_of(q * ROWS, ROWS), ROWS), :]
        total = jnp.zeros((width, LANES), i32)
        for s in range(ROWS):
            total = total + jnp.where(slot_q[s:s + 1, :] == spot, id_q[s:s + 1, :], 0)
        chosen = jnp.sum(total.astype(f32), axis=1, keepdims=True).astype(i32)
        hot = jnp.where(held_iota == chosen, 1.0, 0.0).astype(bf16)
        picked = jnp.dot(hot, book[...], preferred_element_type=f32).astype(bf16)
        rows[q, pl.ds(pl.multiple_of(me * width, width), width), :] = picked
        for s in range(1, owners_x):
            x_copy(q, s).start()
        for s in range(1, cores):
            c_copy(q, s).start()
        return 0

    lax.fori_loop(0, supers, pick, 0)

    load_codes.wait()
    for load in loads[4:]:
        load.wait()
    levels = [bucket_ref[v] for v in range(bucket_ref.shape[0])]
    place_iota = lax.broadcasted_iota(i32, (2 * ROWS, SUPER), 1)

    def prepare(q, _):
        place_q = place[pl.ds(pl.multiple_of(q * ROWS, ROWS), ROWS), :]
        for l in range(0, LANES, 2):
            pair = jnp.concatenate([place_q[:, l:l + 1], place_q[:, l + 1:l + 2]], axis=0)
            perm[q, l * ROWS:(l + 2) * ROWS, :] = jnp.where(place_iota == pair, 1.0, 0.0).astype(bf16)
        for l in range(LANES):
            code = codes[pl.ds(q * SUPER + l, ROWS, stride=LANES), :]
            value = jnp.full(code.shape, levels[0], f32)
            for v in range(1, len(levels)):
                value = jnp.where(code == v, levels[v], value)
            resid[q, l * ROWS:(l + 1) * ROWS, :] = value
        for s in range(1, owners_x):
            source = lax.rem(x + s, owners_x) * cores + c
            x_wait = send(q, source, x_send.at[q, s], (y, z, x, c))
            x_wait.wait_recv()
            for t in range(1, cores):
                relay(q, s, t).start()
        return 0

    lax.fori_loop(0, supers, prepare, 0)

    blocks = supers * 2 * ROWS
    line = lax.broadcasted_iota(i32, (blocks, 1), 0)
    block = 2 * ROWS * (line // (2 * ROWS)) + 2 * (line % ROWS) + (line // ROWS) % 2
    end = jnp.int32(0)
    doc = jnp.zeros((blocks, 1), i32)
    docs = docs_ref.shape[1]
    for d in range(docs):
        end = end + docs_ref[0, d]
        doc = doc + jnp.where(end <= block, 1, 0)

    def score(j, query, q):
        for h in range(2):
            top = None
            for p in range(0, BLOCK * ROWS, 128):
                piece = dec[q, h * BLOCK * ROWS + p:h * BLOCK * ROWS + p + 128, :]
                sim = lax.dot_general(piece, query, (((1,), (1,)), ((), ())), preferred_element_type=f32)
                sim = jnp.max(sim.reshape(-1, ROWS, sim.shape[1]), axis=0)
                top = sim if top is None else jnp.maximum(top, sim)
            best[j, pl.ds(pl.multiple_of(q * 2 * ROWS + h * ROWS, ROWS), ROWS), :] = top

    def decode(q, _):
        for s in range(owners_x):
            for t in range(cores):
                if t == 0:
                    continue
                source = lax.rem(x + s, owners_x) * cores + lax.rem(c + t, cores)
                send(q, source, c_send.at[q, t], (y, z, x, c)).wait_recv()
        vectors = jnp.dot(perm[q], rows[q], preferred_element_type=f32) + resid[q]
        squares = jnp.sum(vectors * vectors, axis=1, keepdims=True)
        dec[q] = (vectors * lax.rsqrt(squares + norm_eps)).astype(bf16)
        score(z, q_ref[...], q)
        return 0

    lax.fori_loop(0, supers, decode, 0)

    panel_rows = q_ref.shape[0]
    queries = out_ref.shape[1]
    tokens = panel_rows // queries
    gather = (
        lax.broadcasted_iota(i32, (queries, panel_rows), 1) // tokens
        == lax.broadcasted_iota(i32, (queries, panel_rows), 0)
    ).astype(f32)
    slot_count = cand_ref.shape[3]
    slot_iota = lax.broadcasted_iota(i32, (1, slot_count), 1)

    def finish(j):
        live = (cand_ref[j, 0] == block) & (slot_iota < counts_ref[j])
        alive = jnp.max(jnp.where(live, 1.0, 0.0), axis=1, keepdims=True) > 0.5
        which = jnp.where(alive, doc, -1)
        maxima = best[j]
        lines = []
        for d in range(docs):
            lines.append(jnp.max(jnp.where(which == d, maxima, floor_value), axis=0, keepdims=True))
        found = jnp.concatenate(lines, axis=0)
        found = jnp.where(found > 0.5 * floor_value, found, 0.0)
        total = lax.dot_general(
            gather, found, (((1,), (1,)), ((), ())),
            preferred_element_type=f32, precision=lax.Precision.HIGHEST,
        )
        out_ref[j] = total * (1.0 / tokens)

    finish(z)

    def panel(s, _):
        j = lax.rem(z + shards - s, shards)
        pltpu.make_async_remote_copy(
            src_ref=q_ref, dst_ref=panels.at[j], send_sem=q_send.at[s], recv_sem=q_recv.at[j],
            device_id=(y, z, x, c), device_id_type=pl.DeviceIdType.MESH,
        ).wait_recv()

        def each(q, _):
            score(j, panels[j], q)
            return 0

        lax.fori_loop(0, supers, each, 0)
        finish(j)
        return 0

    lax.fori_loop(1, shards, panel, 0)

    for s in range(1, shards):
        q_copy(s).wait_send()

    def drain(q, _):
        for s in range(1, owners_x):
            x_copy(q, s).wait_send()
            for t in range(1, cores):
                relay(q, s, t).wait_send()
        for s in range(1, cores):
            c_copy(q, s).wait_send()
        return 0

    lax.fori_loop(0, supers, drain, 0)


def local(shards, owners_x, cores, queries, codebook, bucket_values, token_centroids, residual_codes,
          doc_blocks, cand_blocks, cand_counts):
    count, panel, tokens, depth = queries.shape[0], queries.shape[1], queries.shape[2], queries.shape[3]
    flat_q = queries.reshape(panel * tokens, depth)
    total = token_centroids.shape[0]
    supers = total // SUPER
    held = codebook.shape[0]
    owners = owners_x * cores
    docs = doc_blocks.shape[1]
    vmem, hbm = pl.BlockSpec(memory_space=pltpu.VMEM), pl.BlockSpec(memory_space=pltpu.HBM)
    dma = pltpu.SemaphoreType.DMA
    return pl.pallas_call(
        functools.partial(kernel, shards, owners_x, cores),
        out_shape=jax.ShapeDtypeStruct((shards, panel, docs), f32),
        in_specs=[hbm] * 8,
        out_specs=vmem,
        scratch_shapes=[
            pltpu.VMEM((total // LANES, LANES), i32),
            pltpu.VMEM(cand_blocks.shape, i32),
            pltpu.SMEM((shards,), i32),
            pltpu.SMEM(doc_blocks.shape, i32),
            pltpu.SMEM(bucket_values.shape, f32),
            pltpu.VMEM((panel * tokens, depth), bf16),
            pltpu.VMEM((held, depth), bf16),
            pltpu.VMEM((total, depth), i32),
            pltpu.VMEM((total // LANES, LANES), i32),
            pltpu.VMEM((total // LANES, LANES), i32),
            pltpu.VMEM((total // LANES, LANES), i32),
            pltpu.VMEM((supers, SUPER, depth), bf16),
            pltpu.VMEM((supers, SUPER, SUPER), bf16),
            pltpu.VMEM((supers, SUPER, depth), f32),
            pltpu.VMEM((supers, SUPER, depth), bf16),
            pltpu.VMEM((shards, panel * tokens, depth), bf16),
            pltpu.VMEM((shards, total // BLOCK, panel * tokens), f32),
            dma((8,)),
            dma((shards,)),
            dma((shards,)),
            dma((supers, owners_x)),
            dma((supers, cores)),
            dma((supers, owners_x, cores)),
            dma((supers, owners)),
        ],
        compiler_params=pltpu.CompilerParams(
            collective_id=0, has_side_effects=True, vmem_limit_bytes=64 * 1024 * 1024
        ),
        name="rescore",
    )(
        token_centroids.reshape(total // LANES, LANES), cand_blocks, cand_counts.reshape(shards), doc_blocks,
        bucket_values, flat_q, codebook, residual_codes,
    )


def solution(mesh):
    in_specs = (
        P(("grp", "doc"), ("qry", "dim"), None, None),
        P(("qry", "dim"), None),
        P(),
        P(("grp", "doc")),
        P(("grp", "doc"), None),
        P(("grp", "doc"), None),
        P("grp", ("qry", "dim"), "doc", None),
        P("grp", ("qry", "dim"), "doc"),
    )
    out_specs = P("grp", ("qry", "dim"), "doc")
    body = functools.partial(local, mesh.shape["doc"], mesh.shape["qry"], mesh.shape["dim"])
    return jax.shard_map(body, mesh=mesh, in_specs=in_specs, out_specs=out_specs, check_vma=False)
```

```python
import functools

import jax
import jax.numpy as jnp
from jax import lax
from jax.experimental import pallas as pl
from jax.experimental.pallas import tpu as pltpu
from jax.sharding import PartitionSpec as P

BLOCK = 64
LANES = 128
ROWS = 8
FOLD = 4
SUPER = ROWS * LANES

norm_eps = 1e-06
floor_value = -10000.0
bf16, f32, i32 = jnp.bfloat16, jnp.float32, jnp.int32


def kernel(
    shards, owners_x, cores,
    ids_hbm, cand_hbm, counts_hbm, docs_hbm, bucket_hbm, q_hbm, book_hbm, codes_hbm,
    out_ref,
    ids_ref, cand_ref, counts_ref, docs_ref, bucket_ref, q_ref, book, codes, ranks, place, slots, rows, perm, quarter, resid, dec, panels, best, found,
    load_sem, q_send, q_recv, x_send, c_send, r_send, row_recv,
):
    y, z = lax.axis_index("grp"), lax.axis_index("doc")
    x, c = lax.axis_index("qry"), lax.axis_index("dim")
    owners = owners_x * cores
    me = x * cores + c
    held = book.shape[0]
    supers = codes.shape[0] // SUPER
    width = SUPER // owners
    run_rows = codes.shape[0] // owners // LANES
    part = SUPER // (run_rows * LANES)
    share = width // part
    token_rows = ids_ref.shape[0]

    loads = [
        pltpu.make_async_copy(source, target, load_sem.at[n])
        for n, (source, target) in enumerate([
            (ids_hbm, ids_ref), (q_hbm, q_ref), (book_hbm, book), (codes_hbm, codes), (cand_hbm, cand_ref),
            (counts_hbm, counts_ref), (docs_hbm, docs_ref), (bucket_hbm, bucket_ref),
        ])
    ]
    load_ids, load_q, load_book, load_codes = loads[:4]
    for load in loads:
        load.start()

    barrier = pltpu.get_barrier_semaphore()
    peers = [(y, lax.rem(z + s, shards), x, c) for s in range(1, shards)]
    peers += [(y, z, lax.rem(x + s, owners_x), c) for s in range(1, owners_x)]
    peers += [(y, z, x, lax.rem(c + s, cores)) for s in range(1, cores)]
    for peer in peers:
        pl.semaphore_signal(barrier, inc=1, device_id=peer, device_id_type=pl.DeviceIdType.MESH)

    load_q.wait()
    panels[z] = q_ref[...].T
    pl.semaphore_wait(barrier, len(peers))

    def q_copy(s):
        return pltpu.make_async_remote_copy(
            src_ref=panels.at[z], dst_ref=panels.at[z],
            send_sem=q_send.at[s], recv_sem=q_recv.at[z],
            device_id=(y, lax.rem(z + s, shards), x, c), device_id_type=pl.DeviceIdType.MESH,
        )

    for s in range(1, shards):
        q_copy(s).start()

    load_ids.wait()
    ids = ids_ref[...]
    owner = ids // held
    lane_r = lax.broadcasted_iota(i32, (LANES, LANES), 0)
    lane_c = lax.broadcasted_iota(i32, (LANES, LANES), 1)
    before = (lane_r < lane_c).astype(bf16)
    ones = jnp.ones((LANES, LANES), bf16)
    row_r = lax.broadcasted_iota(i32, (token_rows, token_rows), 0)
    row_c = lax.broadcasted_iota(i32, (token_rows, token_rows), 1)
    above = ((row_c < row_r) & (row_c // run_rows == row_r // run_rows)).astype(bf16)
    rank = jnp.zeros(ids.shape, f32)
    for o in range(owners):
        mask = (owner == o).astype(f32)
        inside = jnp.dot(mask.astype(bf16), before, preferred_element_type=f32)
        totals = jnp.dot(mask.astype(bf16), ones, preferred_element_type=f32)
        carried = jnp.dot(above, totals.astype(bf16), preferred_element_type=f32)
        rank = rank + mask * (inside + carried)
    run_of = (lax.broadcasted_iota(i32, ids.shape, 0) // run_rows) % part
    slot = run_of * share + rank.astype(i32)
    place[...] = owner * width + slot
    slots[...] = jnp.where(owner == me, slot, -1)
    ranks[...] = ids - me * held

    def chunk(q, o):
        return rows.at[q, pl.ds(pl.multiple_of(o * width, width), width), :]

    def send(q, o, sem, device):
        return pltpu.make_async_remote_copy(
            src_ref=chunk(q, o), dst_ref=chunk(q, o), send_sem=sem, recv_sem=row_recv.at[q, o],
            device_id=device, device_id_type=pl.DeviceIdType.MESH,
        )

    def x_copy(q, s):
        return send(q, me, x_send.at[q, s], (y, z, lax.rem(x + s, owners_x), c))

    def c_copy(q, s):
        return send(q, me, c_send.at[q, s], (y, z, x, lax.rem(c + s, cores)))

    def relay(q, s, t):
        source = lax.rem(x + s, owners_x) * cores + c
        return send(q, source, r_send.at[q, s, t], (y, z, x, lax.rem(c + t, cores)))

    load_book.wait()
    spot = lax.broadcasted_iota(i32, (width, LANES), 0)
    piece_held = held // FOLD
    held_iota = lax.broadcasted_iota(i32, (width, piece_held), 1)

    def side_by_side(table):
        size = table.shape[0] // FOLD
        return jnp.concatenate([table[f * size:(f + 1) * size] for f in range(FOLD)], axis=1)

    def of_quarter(wide, which):
        depth = wide.shape[1] // FOLD
        value = wide[:, :depth]
        for f in range(1, FOLD):
            value = jnp.where(which == f, wide[:, f * depth:(f + 1) * depth], value)
        return value

    def pick(q, _):
        slot_q = slots[pl.ds(pl.multiple_of(q * ROWS, ROWS), ROWS), :]
        id_q = ranks[pl.ds(pl.multiple_of(q * ROWS, ROWS), ROWS), :]
        total = jnp.zeros((width, LANES), i32)
        for s in range(ROWS):
            total = total + jnp.where(slot_q[s:s + 1, :] == spot, id_q[s:s + 1, :], 0)
        chosen = jnp.sum(total.astype(f32), axis=1, keepdims=True).astype(i32)
        hot = jnp.where(held_iota == chosen % piece_held, 1.0, 0.0).astype(bf16)
        wide = jnp.dot(hot, side_by_side(book[...]), preferred_element_type=f32)
        picked = of_quarter(wide, chosen // piece_held).astype(bf16)
        rows[q, pl.ds(pl.multiple_of(me * width, width), width), :] = picked
        for s in range(1, owners_x):
            x_copy(q, s).start()
        for s in range(1, cores):
            c_copy(q, s).start()
        return 0

    lax.fori_loop(0, supers, pick, 0)

    load_codes.wait()
    for load in loads[4:]:
        load.wait()
    levels = [bucket_ref[v] for v in range(bucket_ref.shape[0])]
    piece_super = SUPER // FOLD
    place_iota = lax.broadcasted_iota(i32, (2 * ROWS, piece_super), 1)

    def prepare(q, _):
        place_q = place[pl.ds(pl.multiple_of(q * ROWS, ROWS), ROWS), :]
        for l in range(0, LANES, 2):
            pair = jnp.concatenate([place_q[:, l:l + 1], place_q[:, l + 1:l + 2]], axis=0)
            perm[q, l * ROWS:(l + 2) * ROWS, :] = jnp.where(place_iota == pair % piece_super, 1.0, 0.0).astype(bf16)
            quarter[q, l * ROWS:(l + 2) * ROWS, :] = jnp.broadcast_to(pair // piece_super, (2 * ROWS, LANES))
        for l in range(LANES):
            code = codes[pl.ds(q * SUPER + l, ROWS, stride=LANES), :]
            value = jnp.full(code.shape, levels[0], f32)
            for v in range(1, len(levels)):
                value = jnp.where(code == v, levels[v], value)
            resid[q, l * ROWS:(l + 1) * ROWS, :] = value
        for s in range(1, owners_x):
            source = lax.rem(x + s, owners_x) * cores + c
            x_wait = send(q, source, x_send.at[q, s], (y, z, x, c))
            x_wait.wait_recv()
            for t in range(1, cores):
                relay(q, s, t).start()
        return 0

    lax.fori_loop(0, supers, prepare, 0)

    blocks = supers * 2 * ROWS
    line = lax.broadcasted_iota(i32, (blocks, 1), 0)
    block = 2 * ROWS * (line // (2 * ROWS)) + 2 * (line % ROWS) + (line // ROWS) % 2
    end = jnp.int32(0)
    doc = jnp.zeros((blocks, 1), i32)
    docs = docs_ref.shape[1]
    for d in range(docs):
        end = end + docs_ref[0, d]
        doc = doc + jnp.where(end <= block, 1, 0)

    def score(j, query, q):
        for h in range(2):
            top = None
            for p in range(0, BLOCK * ROWS, 128):
                piece = dec[q, h * BLOCK * ROWS + p:h * BLOCK * ROWS + p + 128, :]
                sim = jnp.dot(piece, query, preferred_element_type=f32)
                sim = jnp.max(sim.reshape(-1, ROWS, sim.shape[1]), axis=0)
                top = sim if top is None else jnp.maximum(top, sim)
            best[j, pl.ds(pl.multiple_of(q * 2 * ROWS + h * ROWS, ROWS), ROWS), :] = top

    def decode(q, _):
        for s in range(owners_x):
            for t in range(cores):
                if t == 0:
                    continue
                source = lax.rem(x + s, owners_x) * cores + lax.rem(c + t, cores)
                send(q, source, c_send.at[q, t], (y, z, x, c)).wait_recv()
        wide = jnp.dot(perm[q], side_by_side(rows[q]), preferred_element_type=f32)
        vectors = of_quarter(wide, quarter[q]) + resid[q]
        squares = jnp.sum(vectors * vectors, axis=1, keepdims=True)
        dec[q] = (vectors * lax.rsqrt(squares + norm_eps)).astype(bf16)
        score(z, panels[z], q)
        return 0

    lax.fori_loop(0, supers, decode, 0)

    panel_rows = q_ref.shape[0]
    queries = out_ref.shape[1]
    tokens = panel_rows // queries
    gather = (
        lax.broadcasted_iota(i32, (queries, panel_rows), 1) // tokens
        == lax.broadcasted_iota(i32, (queries, panel_rows), 0)
    ).astype(f32)
    slot_count = cand_ref.shape[3]
    slot_iota = lax.broadcasted_iota(i32, (1, slot_count), 1)

    def finish(j):
        live = (cand_ref[j, 0] == block) & (slot_iota < counts_ref[j])
        alive = jnp.max(jnp.where(live, 1.0, 0.0), axis=1, keepdims=True) > 0.5
        which = jnp.where(alive, doc, -1)
        maxima = best[j]
        lines = []
        for d in range(docs):
            lines.append(jnp.max(jnp.where(which == d, maxima, floor_value), axis=0, keepdims=True))
        tops = jnp.concatenate(lines, axis=0)
        found[j] = jnp.where(tops > 0.5 * floor_value, tops, 0.0)

    def total_up(j):
        total = lax.dot_general(
            gather, found[j], (((1,), (1,)), ((), ())),
            preferred_element_type=f32, precision=lax.Precision.HIGHEST,
        )
        out_ref[j] = total * (1.0 / tokens)

    finish(z)

    def panel(s, _):
        j = lax.rem(z + shards - s, shards)
        pltpu.make_async_remote_copy(
            src_ref=panels.at[z], dst_ref=panels.at[j], send_sem=q_send.at[s], recv_sem=q_recv.at[j],
            device_id=(y, z, x, c), device_id_type=pl.DeviceIdType.MESH,
        ).wait_recv()

        def each(q, _):
            score(j, panels[j], q)
            return 0

        lax.fori_loop(0, supers, each, 0)
        finish(j)
        return 0

    lax.fori_loop(1, shards, panel, 0)

    for j in range(shards):
        total_up(j)

    for s in range(1, shards):
        q_copy(s).wait_send()

    def drain(q, _):
        for s in range(1, owners_x):
            x_copy(q, s).wait_send()
            for t in range(1, cores):
                relay(q, s, t).wait_send()
        for s in range(1, cores):
            c_copy(q, s).wait_send()
        return 0

    lax.fori_loop(0, supers, drain, 0)


def local(shards, owners_x, cores, queries, codebook, bucket_values, token_centroids, residual_codes,
          doc_blocks, cand_blocks, cand_counts):
    count, panel, tokens, depth = queries.shape[0], queries.shape[1], queries.shape[2], queries.shape[3]
    flat_q = queries.reshape(panel * tokens, depth)
    total = token_centroids.shape[0]
    supers = total // SUPER
    held = codebook.shape[0]
    owners = owners_x * cores
    docs = doc_blocks.shape[1]
    vmem, hbm = pl.BlockSpec(memory_space=pltpu.VMEM), pl.BlockSpec(memory_space=pltpu.HBM)
    dma = pltpu.SemaphoreType.DMA
    return pl.pallas_call(
        functools.partial(kernel, shards, owners_x, cores),
        out_shape=jax.ShapeDtypeStruct((shards, panel, docs), f32),
        in_specs=[hbm] * 8,
        out_specs=vmem,
        scratch_shapes=[
            pltpu.VMEM((total // LANES, LANES), i32),
            pltpu.VMEM(cand_blocks.shape, i32),
            pltpu.SMEM((shards,), i32),
            pltpu.SMEM(doc_blocks.shape, i32),
            pltpu.SMEM(bucket_values.shape, f32),
            pltpu.VMEM((panel * tokens, depth), bf16),
            pltpu.VMEM((held, depth), bf16),
            pltpu.VMEM((total, depth), i32),
            pltpu.VMEM((total // LANES, LANES), i32),
            pltpu.VMEM((total // LANES, LANES), i32),
            pltpu.VMEM((total // LANES, LANES), i32),
            pltpu.VMEM((supers, SUPER, depth), bf16),
            pltpu.VMEM((supers, SUPER, SUPER // FOLD), bf16),
            pltpu.VMEM((supers, SUPER, depth), i32),
            pltpu.VMEM((supers, SUPER, depth), f32),
            pltpu.VMEM((supers, SUPER, depth), bf16),
            pltpu.VMEM((shards, depth, panel * tokens), bf16),
            pltpu.VMEM((shards, total // BLOCK, panel * tokens), f32),
            pltpu.VMEM((shards, docs, panel * tokens), f32),
            dma((8,)),
            dma((shards,)),
            dma((shards,)),
            dma((supers, owners_x)),
            dma((supers, cores)),
            dma((supers, owners_x, cores)),
            dma((supers, owners)),
        ],
        compiler_params=pltpu.CompilerParams(
            collective_id=0, has_side_effects=True, vmem_limit_bytes=64 * 1024 * 1024
        ),
        name="rescore",
    )(
        token_centroids.reshape(total // LANES, LANES), cand_blocks, cand_counts.reshape(shards), doc_blocks,
        bucket_values, flat_q, codebook, residual_codes,
    )


def solution(mesh):
    in_specs = (
        P(("grp", "doc"), ("qry", "dim"), None, None),
        P(("qry", "dim"), None),
        P(),
        P(("grp", "doc")),
        P(("grp", "doc"), None),
        P(("grp", "doc"), None),
        P("grp", ("qry", "dim"), "doc", None),
        P("grp", ("qry", "dim"), "doc"),
    )
    out_specs = P("grp", ("qry", "dim"), "doc")
    body = functools.partial(local, mesh.shape["doc"], mesh.shape["qry"], mesh.shape["dim"])
    return jax.shard_map(body, mesh=mesh, in_specs=in_specs, out_specs=out_specs, check_vma=False)
```

```python
import functools

import jax
import jax.numpy as jnp
from jax import lax
from jax.experimental import pallas as pl
from jax.experimental.pallas import tpu as pltpu
from jax.sharding import PartitionSpec as P

BLOCK = 64
LANES = 128
ROWS = 8
FOLD = 4
SUPER = ROWS * LANES

norm_eps = 1e-06
floor_value = -10000.0
bf16, f32, i32 = jnp.bfloat16, jnp.float32, jnp.int32


def kernel(
    shards, owners_x, cores,
    ids_hbm, cand_hbm, counts_hbm, docs_hbm, bucket_hbm, q_hbm, book_hbm, codes_hbm,
    out_ref,
    ids_ref, cand_ref, counts_ref, docs_ref, bucket_ref, q_ref, book, codes, ranks, place, slots, rows, perm, quarter, resid, dec, panels, best, found,
    load_sem, q_send, q_recv, x_send, c_send, r_send, row_recv,
):
    bits = [1 << n for n in range(shards.bit_length() - 1)]
    y, z = lax.axis_index("grp"), lax.axis_index("doc")
    x, c = lax.axis_index("qry"), lax.axis_index("dim")
    owners = owners_x * cores
    me = x * cores + c
    held = book.shape[0]
    supers = codes.shape[0] // SUPER
    width = SUPER // owners
    run_rows = codes.shape[0] // owners // LANES
    part = SUPER // (run_rows * LANES)
    share = width // part
    token_rows = ids_ref.shape[0]

    loads = [
        pltpu.make_async_copy(source, target, load_sem.at[n])
        for n, (source, target) in enumerate([
            (ids_hbm, ids_ref), (q_hbm, q_ref), (book_hbm, book), (codes_hbm, codes), (cand_hbm, cand_ref),
            (counts_hbm, counts_ref), (docs_hbm, docs_ref), (bucket_hbm, bucket_ref),
        ])
    ]
    load_ids, load_q, load_book, load_codes = loads[:4]
    for load in loads:
        load.start()

    barrier = pltpu.get_barrier_semaphore()
    peers = [(y, lax.rem(z + s, shards), x, c) for s in range(1, shards)]
    peers += [(y, z, lax.rem(x + s, owners_x), c) for s in range(1, owners_x)]
    peers += [(y, z, x, lax.rem(c + s, cores)) for s in range(1, cores)]
    for peer in peers:
        pl.semaphore_signal(barrier, inc=1, device_id=peer, device_id_type=pl.DeviceIdType.MESH)

    load_q.wait()
    panels[z] = q_ref[...].T
    pl.semaphore_wait(barrier, len(peers))

    def partner(s):
        return sum(((z // bit + s // bit) % 2) * bit for bit in bits)

    def q_copy(s):
        return pltpu.make_async_remote_copy(
            src_ref=panels.at[z], dst_ref=panels.at[z],
            send_sem=q_send.at[s], recv_sem=q_recv.at[z],
            device_id=(y, partner(s), x, c), device_id_type=pl.DeviceIdType.MESH,
        )

    for s in range(1, shards):
        q_copy(s).start()

    load_ids.wait()
    ids = ids_ref[...]
    owner = ids // held
    lane_r = lax.broadcasted_iota(i32, (LANES, LANES), 0)
    lane_c = lax.broadcasted_iota(i32, (LANES, LANES), 1)
    before = (lane_r < lane_c).astype(bf16)
    ones = jnp.ones((LANES, LANES), bf16)
    row_r = lax.broadcasted_iota(i32, (token_rows, token_rows), 0)
    row_c = lax.broadcasted_iota(i32, (token_rows, token_rows), 1)
    above = ((row_c < row_r) & (row_c // run_rows == row_r // run_rows)).astype(bf16)
    rank = jnp.zeros(ids.shape, f32)
    for o in range(owners):
        mask = (owner == o).astype(f32)
        inside = jnp.dot(mask.astype(bf16), before, preferred_element_type=f32)
        totals = jnp.dot(mask.astype(bf16), ones, preferred_element_type=f32)
        carried = jnp.dot(above, totals.astype(bf16), preferred_element_type=f32)
        rank = rank + mask * (inside + carried)
    run_of = (lax.broadcasted_iota(i32, ids.shape, 0) // run_rows) % part
    slot = run_of * share + rank.astype(i32)
    place[...] = owner * width + slot
    slots[...] = jnp.where(owner == me, slot, -1)
    ranks[...] = ids - me * held

    def chunk(q, o):
        return rows.at[q, pl.ds(pl.multiple_of(o * width, width), width), :]

    def send(q, o, sem, device):
        return pltpu.make_async_remote_copy(
            src_ref=chunk(q, o), dst_ref=chunk(q, o), send_sem=sem, recv_sem=row_recv.at[q, o],
            device_id=device, device_id_type=pl.DeviceIdType.MESH,
        )

    def x_copy(q, s):
        return send(q, me, x_send.at[q, s], (y, z, lax.rem(x + s, owners_x), c))

    def c_copy(q, s):
        return send(q, me, c_send.at[q, s], (y, z, x, lax.rem(c + s, cores)))

    def relay(q, s, t):
        source = lax.rem(x + s, owners_x) * cores + c
        return send(q, source, r_send.at[q, s, t], (y, z, x, lax.rem(c + t, cores)))

    load_book.wait()
    spot = lax.broadcasted_iota(i32, (width, LANES), 0)
    piece_held = held // FOLD
    held_iota = lax.broadcasted_iota(i32, (width, piece_held), 1)

    def side_by_side(table):
        size = table.shape[0] // FOLD
        return jnp.concatenate([table[f * size:(f + 1) * size] for f in range(FOLD)], axis=1)

    def of_quarter(wide, which):
        depth = wide.shape[1] // FOLD
        value = wide[:, :depth]
        for f in range(1, FOLD):
            value = jnp.where(which == f, wide[:, f * depth:(f + 1) * depth], value)
        return value

    def pick(q, _):
        slot_q = slots[pl.ds(pl.multiple_of(q * ROWS, ROWS), ROWS), :]
        id_q = ranks[pl.ds(pl.multiple_of(q * ROWS, ROWS), ROWS), :]
        total = jnp.zeros((width, LANES), i32)
        for s in range(ROWS):
            total = total + jnp.where(slot_q[s:s + 1, :] == spot, id_q[s:s + 1, :], 0)
        chosen = jnp.sum(total.astype(f32), axis=1, keepdims=True).astype(i32)
        hot = jnp.where(held_iota == chosen % piece_held, 1.0, 0.0).astype(bf16)
        wide = jnp.dot(hot, side_by_side(book[...]), preferred_element_type=f32)
        picked = of_quarter(wide, chosen // piece_held).astype(bf16)
        rows[q, pl.ds(pl.multiple_of(me * width, width), width), :] = picked
        for s in range(1, owners_x):
            x_copy(q, s).start()
        for s in range(1, cores):
            c_copy(q, s).start()
        return 0

    lax.fori_loop(0, supers, pick, 0)

    load_codes.wait()
    for load in loads[4:]:
        load.wait()
    levels = [bucket_ref[v] for v in range(bucket_ref.shape[0])]
    piece_super = SUPER // FOLD
    place_iota = lax.broadcasted_iota(i32, (2 * ROWS, piece_super), 1)

    def prepare(q, _):
        place_q = place[pl.ds(pl.multiple_of(q * ROWS, ROWS), ROWS), :]
        for l in range(0, LANES, 2):
            pair = jnp.concatenate([place_q[:, l:l + 1], place_q[:, l + 1:l + 2]], axis=0)
            perm[q, l * ROWS:(l + 2) * ROWS, :] = jnp.where(place_iota == pair % piece_super, 1.0, 0.0).astype(bf16)
            quarter[q, l * ROWS:(l + 2) * ROWS, :] = jnp.broadcast_to(pair // piece_super, (2 * ROWS, LANES))
        for l in range(LANES):
            code = codes[pl.ds(q * SUPER + l, ROWS, stride=LANES), :]
            value = jnp.full(code.shape, levels[0], f32)
            for v in range(1, len(levels)):
                value = jnp.where(code == v, levels[v], value)
            resid[q, l * ROWS:(l + 1) * ROWS, :] = value
        return 0

    def pass_on(q):
        for s in range(1, owners_x):
            source = lax.rem(x + s, owners_x) * cores + c
            send(q, source, x_send.at[q, s], (y, z, x, c)).wait_recv()
            for t in range(1, cores):
                relay(q, s, t).start()

    def prepare_and_pass(q, _):
        prepare(q, 0)
        pass_on(q - lead)
        return 0

    lead = min(2, supers)
    lax.fori_loop(0, lead, prepare, 0)
    lax.fori_loop(lead, supers, prepare_and_pass, 0)

    blocks = supers * 2 * ROWS
    line = lax.broadcasted_iota(i32, (blocks, 1), 0)
    block = 2 * ROWS * (line // (2 * ROWS)) + 2 * (line % ROWS) + (line // ROWS) % 2
    end = jnp.int32(0)
    doc = jnp.zeros((blocks, 1), i32)
    docs = docs_ref.shape[1]
    for d in range(docs):
        end = end + docs_ref[0, d]
        doc = doc + jnp.where(end <= block, 1, 0)

    def score(j, query, q):
        for h in range(2):
            top = None
            for p in range(0, BLOCK * ROWS, 128):
                piece = dec[q, h * BLOCK * ROWS + p:h * BLOCK * ROWS + p + 128, :]
                sim = jnp.dot(piece, query, preferred_element_type=f32)
                sim = jnp.max(sim.reshape(-1, ROWS, sim.shape[1]), axis=0)
                top = sim if top is None else jnp.maximum(top, sim)
            at = q * 2 * ROWS + h * ROWS
            best[j, pl.ds(at if isinstance(at, int) else pl.multiple_of(at, ROWS), ROWS), :] = top

    def panel_arrival(j):
        pltpu.make_async_remote_copy(
            src_ref=panels.at[z], dst_ref=panels.at[j], send_sem=q_send.at[0], recv_sem=q_recv.at[j],
            device_id=(y, z, x, c), device_id_type=pl.DeviceIdType.MESH,
        ).wait_recv()

    def decode(q, _):
        for s in range(owners_x):
            for t in range(cores):
                if t == 0:
                    continue
                source = lax.rem(x + s, owners_x) * cores + lax.rem(c + t, cores)
                send(q, source, c_send.at[q, t], (y, z, x, c)).wait_recv()
        wide = jnp.dot(perm[q], side_by_side(rows[q]), preferred_element_type=f32)
        vectors = of_quarter(wide, quarter[q]) + resid[q]
        squares = jnp.sum(vectors * vectors, axis=1, keepdims=True)
        dec[q] = (vectors * lax.rsqrt(squares + norm_eps)).astype(bf16)
        score(z, panels[z], q)
        score(near, panels[near], q)
        return 0

    def decode_and_pass(q, _):
        decode(q, 0)
        pass_on(q + supers - lead)
        return 0

    near = partner(1)
    panel_arrival(near)
    lax.fori_loop(0, lead, decode_and_pass, 0)
    lax.fori_loop(lead, supers, decode, 0)

    panel_rows = q_ref.shape[0]
    queries = out_ref.shape[1]
    tokens = panel_rows // queries
    gather = (
        lax.broadcasted_iota(i32, (queries, panel_rows), 1) // tokens
        == lax.broadcasted_iota(i32, (queries, panel_rows), 0)
    ).astype(f32)
    slot_count = cand_ref.shape[3]
    slot_iota = lax.broadcasted_iota(i32, (1, slot_count), 1)

    def finish(j):
        live = (cand_ref[j, 0] == block) & (slot_iota < counts_ref[j])
        alive = jnp.max(jnp.where(live, 1.0, 0.0), axis=1, keepdims=True) > 0.5
        which = jnp.where(alive, doc, -1)
        maxima = best[j]
        lines = []
        for d in range(docs):
            lines.append(jnp.max(jnp.where(which == d, maxima, floor_value), axis=0, keepdims=True))
        tops = jnp.concatenate(lines, axis=0)
        found[j] = jnp.where(tops > 0.5 * floor_value, tops, 0.0)

    def total_up(j):
        total = lax.dot_general(
            gather, found[j], (((1,), (1,)), ((), ())),
            preferred_element_type=f32, precision=lax.Precision.HIGHEST,
        )
        out_ref[j] = total * (1.0 / tokens)

    finish(z)

    def panel(s, _):
        j = partner(s)
        panel_arrival(j)
        for q in range(supers):
            score(j, panels[j], q)
        finish(partner(s - 1))
        return 0

    lax.fori_loop(2, shards, panel, 0)
    finish(partner(shards - 1))

    for j in range(shards):
        total_up(j)

    for s in range(1, shards):
        q_copy(s).wait_send()

    def drain(q, _):
        for s in range(1, owners_x):
            x_copy(q, s).wait_send()
            for t in range(1, cores):
                relay(q, s, t).wait_send()
        for s in range(1, cores):
            c_copy(q, s).wait_send()
        return 0

    lax.fori_loop(0, supers, drain, 0)


def local(shards, owners_x, cores, queries, codebook, bucket_values, token_centroids, residual_codes,
          doc_blocks, cand_blocks, cand_counts):
    count, panel, tokens, depth = queries.shape[0], queries.shape[1], queries.shape[2], queries.shape[3]
    flat_q = queries.reshape(panel * tokens, depth)
    total = token_centroids.shape[0]
    supers = total // SUPER
    held = codebook.shape[0]
    owners = owners_x * cores
    docs = doc_blocks.shape[1]
    vmem, hbm = pl.BlockSpec(memory_space=pltpu.VMEM), pl.BlockSpec(memory_space=pltpu.HBM)
    dma = pltpu.SemaphoreType.DMA
    return pl.pallas_call(
        functools.partial(kernel, shards, owners_x, cores),
        out_shape=jax.ShapeDtypeStruct((shards, panel, docs), f32),
        in_specs=[hbm] * 8,
        out_specs=vmem,
        scratch_shapes=[
            pltpu.VMEM((total // LANES, LANES), i32),
            pltpu.VMEM(cand_blocks.shape, i32),
            pltpu.SMEM((shards,), i32),
            pltpu.SMEM(doc_blocks.shape, i32),
            pltpu.SMEM(bucket_values.shape, f32),
            pltpu.VMEM((panel * tokens, depth), bf16),
            pltpu.VMEM((held, depth), bf16),
            pltpu.VMEM((total, depth), i32),
            pltpu.VMEM((total // LANES, LANES), i32),
            pltpu.VMEM((total // LANES, LANES), i32),
            pltpu.VMEM((total // LANES, LANES), i32),
            pltpu.VMEM((supers, SUPER, depth), bf16),
            pltpu.VMEM((supers, SUPER, SUPER // FOLD), bf16),
            pltpu.VMEM((supers, SUPER, depth), i32),
            pltpu.VMEM((supers, SUPER, depth), f32),
            pltpu.VMEM((supers, SUPER, depth), bf16),
            pltpu.VMEM((shards, depth, panel * tokens), bf16),
            pltpu.VMEM((shards, total // BLOCK, panel * tokens), f32),
            pltpu.VMEM((shards, docs, panel * tokens), f32),
            dma((8,)),
            dma((shards,)),
            dma((shards,)),
            dma((supers, owners_x)),
            dma((supers, cores)),
            dma((supers, owners_x, cores)),
            dma((supers, owners)),
        ],
        compiler_params=pltpu.CompilerParams(
            collective_id=0, has_side_effects=True, vmem_limit_bytes=64 * 1024 * 1024
        ),
        name="rescore",
    )(
        token_centroids.reshape(total // LANES, LANES), cand_blocks, cand_counts.reshape(shards), doc_blocks,
        bucket_values, flat_q, codebook, residual_codes,
    )


def solution(mesh):
    in_specs = (
        P(("grp", "doc"), ("qry", "dim"), None, None),
        P(("qry", "dim"), None),
        P(),
        P(("grp", "doc")),
        P(("grp", "doc"), None),
        P(("grp", "doc"), None),
        P("grp", ("qry", "dim"), "doc", None),
        P("grp", ("qry", "dim"), "doc"),
    )
    out_specs = P("grp", ("qry", "dim"), "doc")
    body = functools.partial(local, mesh.shape["doc"], mesh.shape["qry"], mesh.shape["dim"])
    return jax.shard_map(body, mesh=mesh, in_specs=in_specs, out_specs=out_specs, check_vma=False)
```
